32 devices in a mesh: grp: 2 (over x), pix: 16 (over z, y, core).
Axes of the slice: x: 2, y: 2, z: 4, core: 2. Of those that a mesh axis runs over, the one named last changes fastest.
Arguments:
- fields: bfloat16 [2, 2, 128, 512, 512], P('grp', None, None, 'pix'), may hold values from -6 to 6
- lens_phase: float32 [512, 512], P('pix'), may hold values from -3.140625 to 3.140625
- occupancy: float32 [256], replicated, may hold values from 0.05 to 1
- focus_scale: float32 [256], replicated, may hold values from 0.5 to 1.5
- assignment: int32 [256], replicated, may hold values from 0 to 255, each once
- start_basis: float32 [2, 256, 128], replicated, may hold values from -6 to 6
Outputs:
- coherent_modes: bfloat16 [2, 128, 512, 512], P(None, None, 'pix', 'grp')
- relative_power: float32 [128], replicated
The draws below stay inside these ranges and needn't reach their ends.
Inputs may be any that keep to these rules, and one draw needn't show every extreme that they name: `assignment`: each electron is carried by exactly one wavefront slot.
All inputs are finite; a program needn't handle non-finite values.
Results may differ from the reference program's by a relative error of at most 0.0018.
The reference program's roundings to bfloat16 on the way count: a program that leaves them out, or rounds other values in their place, can miss the bound.
Values may be sent and summed in bfloat16 or wider, within the bound.
A program may use at most 128 MiB of HBM per device.

```python
import math
import jax
import jax.numpy as jnp
from jax import lax

NROW = 512
NCOL = 512
MODES = 128
RANK = 128
STEPS = 2
STACK = 256
ELECTRONS = 256
N_GRP = 2


def draw_fields(key, part):
    shared_count = 32
    key_shared = jax.random.fold_in(key, 11)
    key_coeff = jax.random.fold_in(key, 12)
    key_noise = jax.random.fold_in(key, 13)
    decay = 0.8
    shared = jax.random.normal(key_shared, (2, shared_count, NROW * NCOL), jnp.float32)
    noise_level = 0.3
    order = jnp.arange(shared_count, dtype=jnp.float32)
    weights = decay ** order
    coeff = jax.random.normal(key_coeff, (2, N_GRP * MODES, shared_count), jnp.float32) * weights[None, None, :] * 0.70710678
    mixed_re = jnp.dot(coeff[0], shared[0]) - jnp.dot(coeff[1], shared[1])
    mixed_im = jnp.dot(coeff[0], shared[1]) + jnp.dot(coeff[1], shared[0])
    noise = jax.random.normal(key_noise, (2, N_GRP * MODES, NROW * NCOL), jnp.float32)
    total = jnp.sum(weights * weights)
    norm = 1.0 / jnp.sqrt(total + noise_level * noise_level)
    values = (jnp.stack([mixed_re, mixed_im]) + noise_level * noise) * norm
    values = jnp.clip(values, -6.0, 6.0)
    values = values.reshape(2, N_GRP, MODES, NROW, NCOL)
    return jnp.swapaxes(values, 0, 1).astype(jnp.bfloat16)


def normal_values(rng, shape, scale, limit, kind=jnp.bfloat16):
    return jnp.clip(scale * jax.random.normal(rng, shape, jnp.float32), -limit, limit).astype(kind)


def setup_inputs(seed: int = 0) -> dict:
    key_list = jax.random.split(jax.random.key(seed), 7)
    fields = draw_fields(jax.random.fold_in(key_list[6], 71), 0)
    lens_phase = jnp.clip(jax.random.uniform(key_list[1], (NROW, NCOL), jnp.float32, -3.140625, 3.140625), -3.140625, 3.140625)
    occupancy = jnp.clip(jnp.exp(jax.random.uniform(key_list[2], (ELECTRONS,), jnp.float32, math.log(0.05), math.log(1.0))), 0.05, 1.0)
    focus_scale = jnp.clip(jax.random.uniform(key_list[3], (ELECTRONS,), jnp.float32, 0.5, 1.5), 0.5, 1.5)
    assignment = jax.random.permutation(key_list[4], ELECTRONS).astype(jnp.int32)
    start_basis = normal_values(key_list[5], (2, STACK, RANK), 1.0, 6.0, jnp.float32)
    return dict(fields=fields, lens_phase=lens_phase, occupancy=occupancy, focus_scale=focus_scale, assignment=assignment, start_basis=start_basis)


def dft_tables(length):
    index = jnp.arange(length, dtype=jnp.int32)
    product = index[:, None] * index[None, :] % length
    angle = product.astype(jnp.float32) * (2.0 * math.pi / length)
    factor = 1.0 / math.sqrt(length)
    return ((jnp.cos(angle) * factor).astype(jnp.bfloat16), (jnp.sin(angle) * factor).astype(jnp.bfloat16))

def transform_last(stacked, cosine, sine):
    values = stacked.astype(jnp.float32)
    with_cos = jnp.dot(values, cosine.astype(jnp.float32), precision=lax.Precision.HIGHEST)
    with_sin = jnp.dot(values, sine.astype(jnp.float32), precision=lax.Precision.HIGHEST)
    real_part = with_cos[0] + with_sin[1]
    imag_part = with_cos[1] - with_sin[0]
    return jnp.stack([real_part, imag_part]).astype(jnp.bfloat16)

def reference(fields, lens_phase, occupancy, focus_scale, assignment, start_basis):
    highest = lax.Precision.HIGHEST
    cos_cols, sin_cols = dft_tables(NCOL)
    cos_rows, sin_rows = dft_tables(NROW)
    stacks = []
    for group_index in range(N_GRP):
        electron = assignment[group_index * MODES:(group_index + 1) * MODES]
        amplitude = jnp.sqrt(occupancy[electron])[:, None, None]
        angle = focus_scale[electron][:, None, None] * lens_phase[None]
        cosine = jnp.cos(angle)
        sine = jnp.sin(angle)
        field_re = fields[group_index, 0].astype(jnp.float32)
        field_im = fields[group_index, 1].astype(jnp.float32)
        phased = jnp.stack([amplitude * (field_re * cosine - field_im * sine), amplitude * (field_re * sine + field_im * cosine)]).astype(jnp.bfloat16)
        across = transform_last(phased, cos_cols, sin_cols)
        across = jnp.swapaxes(across, 2, 3)
        stacks.append(transform_last(across, cos_rows, sin_rows))
    stack = jnp.concatenate(stacks, axis=1)
    flat = stack.reshape(2, STACK, NCOL * NROW).astype(jnp.float32)
    gram_re = jnp.dot(flat[0], flat[0].T, precision=highest) + jnp.dot(flat[1], flat[1].T, precision=highest)
    gram_im = jnp.dot(flat[0], flat[1].T, precision=highest) - jnp.dot(flat[1], flat[0].T, precision=highest)
    basis_re = start_basis[0]
    basis_im = start_basis[1]
    for iteration in range(STEPS):
        image_re = jnp.dot(gram_re, basis_re, precision=highest) - jnp.dot(gram_im, basis_im, precision=highest)
        image_im = jnp.dot(gram_re, basis_im, precision=highest) + jnp.dot(gram_im, basis_re, precision=highest)
        column_norm = jnp.sqrt(lax.optimization_barrier(jnp.sum(image_re * image_re + image_im * image_im, axis=0)) + 1e-06)
        basis_re = image_re / column_norm[None, :]
        basis_im = image_im / column_norm[None, :]
    rounded = jnp.stack([basis_re, basis_im]).astype(jnp.bfloat16).astype(jnp.float32)
    mode_re = jnp.dot(rounded[0].T, flat[0], precision=highest) - jnp.dot(rounded[1].T, flat[1], precision=highest)
    mode_im = jnp.dot(rounded[0].T, flat[1], precision=highest) + jnp.dot(rounded[1].T, flat[0], precision=highest)
    energy = lax.optimization_barrier(jnp.sum(mode_re * mode_re + mode_im * mode_im, axis=1))
    trace = jnp.sum(jnp.diagonal(gram_re))
    relative_power = energy * STACK / trace
    inverse = lax.rsqrt(energy / (NROW * NCOL) + 1e-06)
    coherent_modes = (jnp.stack([mode_re, mode_im]) * inverse[None, :, None]).astype(jnp.bfloat16)
    return (coherent_modes.reshape(2, RANK, NCOL, NROW), relative_power)
```

```python
import math

import jax
import jax.numpy as jnp
from jax import lax
from jax.sharding import PartitionSpec as P

NROW = 512
NCOL = 512
STEPS = 2


def partner_2(array, axis, apart):
    return lax.ppermute(array, axis, [(i, i ^ 1 << apart) for i in range(lax.axis_size(axis))])


def dft_tables(length):
    index = jnp.arange(length, dtype=jnp.int32)
    product = index[:, None] * index[None, :] % length
    angle = product.astype(jnp.float32) * (2.0 * math.pi / length)
    factor = 1.0 / math.sqrt(length)
    return (
        (jnp.cos(angle) * factor).astype(jnp.bfloat16),
        (jnp.sin(angle) * factor).astype(jnp.bfloat16),
    )


def local(fields, lens_phase, occupancy, focus_scale, assignment, start_basis):
    highest = lax.Precision.HIGHEST
    local_fields = fields[0]
    modes = local_fields.shape[1]
    group_index = lax.axis_index("grp")
    electron = lax.dynamic_slice_in_dim(assignment, group_index * modes, modes)
    choose = (
        electron[:, None] == jnp.arange(assignment.shape[0], dtype=jnp.int32)[None, :]
    ).astype(jnp.float32)
    amplitude = jnp.sqrt(jnp.sum(choose * occupancy[None, :], axis=1))[:, None, None]
    chromatic = jnp.sum(choose * focus_scale[None, :], axis=1)
    angle = chromatic[:, None, None] * lens_phase[None]
    cosine = jnp.cos(angle)
    sine = jnp.sin(angle)
    field_re = local_fields[0].astype(jnp.float32)
    field_im = local_fields[1].astype(jnp.float32)
    phased = jnp.stack(
        [
            amplitude * (field_re * cosine - field_im * sine),
            amplitude * (field_re * sine + field_im * cosine),
        ]
    ).astype(jnp.bfloat16)
    cos_cols, sin_cols = dft_tables(lens_phase.shape[1])
    col_cos = jnp.einsum("zmrc,ck->zmkr", phased, cos_cols, preferred_element_type=jnp.float32)
    col_sin = jnp.einsum("zmrc,ck->zmkr", phased, sin_cols, preferred_element_type=jnp.float32)
    across = jnp.stack([col_cos[0] + col_sin[1], col_cos[1] - col_sin[0]]).astype(jnp.bfloat16)
    full_rows = across.shape[3] * lax.axis_size("pix")
    cos_rows, sin_rows = dft_tables(full_rows)
    pieces = lax.all_to_all(across, "pix", split_axis=2, concat_axis=3, tiled=True)
    half_rows = full_rows // lax.axis_size("grp")
    cos_rows = jnp.roll(cos_rows, -group_index * half_rows, axis=1)
    sin_rows = jnp.roll(sin_rows, -group_index * half_rows, axis=1)

    def row_transform(first):
        cos_part = cos_rows[:, first:first + half_rows]
        sin_part = sin_rows[:, first:first + half_rows]
        row_cos = jnp.dot(pieces, cos_part, preferred_element_type=jnp.float32)
        row_sin = jnp.dot(pieces, sin_part, preferred_element_type=jnp.float32)
        return jnp.stack([row_cos[0] + row_sin[1], row_cos[1] - row_sin[0]]).astype(jnp.bfloat16)

    stack_size = modes * lax.axis_size("grp")
    partner = partner_2(row_transform(half_rows), "grp", 0)
    owned = jnp.concatenate([row_transform(0), partner], axis=1)
    flat = owned.reshape(2, stack_size, -1)
    blocks = jnp.einsum("xap,ybp->xyab", flat, flat, preferred_element_type=jnp.float32)
    local_re = blocks[0, 0] + blocks[1, 1]
    local_im = blocks[0, 1] - blocks[1, 0]

    def ordered(block):
        return jnp.where(group_index == 0, block, jnp.roll(block, (modes, modes), (0, 1)))

    gram_re, gram_im = lax.psum((ordered(local_re), ordered(local_im)), ("grp", "pix"))
    basis_re = start_basis[0]
    basis_im = start_basis[1]
    for iteration in range(STEPS):
        image_re = jnp.dot(gram_re, basis_re, precision=highest) - jnp.dot(
            gram_im, basis_im, precision=highest
        )
        image_im = jnp.dot(gram_re, basis_im, precision=highest) + jnp.dot(
            gram_im, basis_re, precision=highest
        )
        column_norm = jnp.sqrt(jnp.sum(image_re * image_re + image_im * image_im, axis=0) + 1e-06)
        basis_re = image_re / column_norm[None, :]
        basis_im = image_im / column_norm[None, :]
    rounded = jnp.stack([basis_re, basis_im]).astype(jnp.bfloat16)
    rank = rounded.shape[2]
    local_rounded = jnp.where(group_index == 0, rounded, jnp.roll(rounded, modes, 1))
    owned_flat = owned.reshape(2, stack_size, -1)
    products = jnp.einsum("xsk,ysp->xykp", local_rounded, owned_flat, preferred_element_type=jnp.float32)
    mode_re = products[0, 0] - products[1, 1]
    mode_im = products[0, 1] + products[1, 0]
    coeff_re = rounded[0].astype(jnp.float32)
    coeff_im = rounded[1].astype(jnp.float32)
    weighted_re = jnp.dot(gram_re, coeff_re, precision=highest) - jnp.dot(
        gram_im, coeff_im, precision=highest
    )
    weighted_im = jnp.dot(gram_re, coeff_im, precision=highest) + jnp.dot(
        gram_im, coeff_re, precision=highest
    )
    energy = jnp.sum(coeff_re * weighted_re + coeff_im * weighted_im, axis=0)
    trace = jnp.sum(jnp.diagonal(gram_re))
    relative_power = energy * stack_size / trace
    inverse = lax.rsqrt(energy / (NROW * NCOL) + 1e-06)
    coherent_modes = (jnp.stack([mode_re, mode_im]) * inverse[None, :, None]).astype(jnp.bfloat16)
    return (coherent_modes.reshape(2, rank, owned.shape[2], owned.shape[3]), relative_power)


def solution(mesh):
    in_specs = (P("grp", None, None, "pix", None), P("pix", None), P(), P(), P(), P())
    out_specs = (P(None, None, "pix", "grp"), P())
    return jax.shard_map(local, mesh=mesh, in_specs=in_specs, out_specs=out_specs, check_vma=False)
```

```python
import functools
import math

import jax
import jax.numpy as jnp
from jax import lax
from jax.experimental import pallas as pl
from jax.experimental.pallas import tpu as pltpu
from jax.sharding import PartitionSpec as P

NROW = 512
NCOL = 512
STEPS = 2


def partner_2(array, axis, apart):
    return lax.ppermute(array, axis, [(i, i ^ 1 << apart) for i in range(lax.axis_size(axis))])


def dft_tables(length):
    index = jnp.arange(length, dtype=jnp.int32)
    product = index[:, None] * index[None, :] % length
    angle = product.astype(jnp.float32) * (2.0 * math.pi / length)
    factor = 1.0 / math.sqrt(length)
    return (
        (jnp.cos(angle) * factor).astype(jnp.bfloat16),
        (jnp.sin(angle) * factor).astype(jnp.bfloat16),
    )


MESH = pl.DeviceIdType.MESH


def place(flat, pix_size):
    return (flat // pix_size, lax.rem(flat, pix_size))


def greet(me, total, pix_size):
    barrier = pltpu.get_barrier_semaphore()

    def hello(step, carry):
        other = lax.rem(me + step, total)
        pl.semaphore_signal(barrier, inc=1, device_id=place(other, pix_size), device_id_type=MESH)
        return carry

    lax.fori_loop(1, total, hello, 0)
    pl.semaphore_wait(barrier, total - 1)


def all_reduce(me, total, pix_size, part, landed, result, sems):
    def scatter(step):
        other = lax.rem(me + step, total)
        return pltpu.make_async_remote_copy(
            src_ref=part.at[other],
            dst_ref=landed.at[step],
            send_sem=sems.at[0, step],
            recv_sem=sems.at[1, step],
            device_id=place(other, pix_size),
            device_id_type=MESH,
        )

    def gather(step):
        other = lax.rem(me + step, total)
        return pltpu.make_async_remote_copy(
            src_ref=result.at[me],
            dst_ref=result.at[me],
            send_sem=sems.at[2, step],
            recv_sem=sems.at[3, step],
            device_id=place(other, pix_size),
            device_id_type=MESH,
        )

    def start_scatter(step, carry):
        scatter(step).start()
        return carry

    def add_one(step, sum_so_far):
        scatter(step).wait_recv()
        return sum_so_far + landed[step]

    def start_gather(step, carry):
        gather(step).start()
        return carry

    def finish(step, carry):
        scatter(step).wait_send()
        gather(step).wait_send()
        source = lax.rem(me - step + total, total)
        pltpu.make_async_remote_copy(
            src_ref=result.at[me],
            dst_ref=result.at[source],
            send_sem=sems.at[2, step],
            recv_sem=sems.at[3, step],
            device_id=place(source, pix_size),
            device_id_type=MESH,
        ).wait_recv()
        return carry

    lax.fori_loop(1, total, start_scatter, 0)
    result[me] = lax.fori_loop(1, total, add_one, part[me])
    lax.fori_loop(1, total, start_gather, 0)
    lax.fori_loop(1, total, finish, 0)


def reduce_kernel(grp_size, pix_size, part, result, landed, sems):
    total = grp_size * pix_size
    me = lax.axis_index("grp") * pix_size + lax.axis_index("pix")
    greet(me, total, pix_size)
    all_reduce(me, total, pix_size, part, landed, result, sems)


def sum_over_devices(packed):
    grp_size, pix_size = lax.axis_size("grp"), lax.axis_size("pix")
    total = grp_size * pix_size
    rows, columns = packed.shape
    shape = (total, rows // total, columns)
    out = pl.pallas_call(
        functools.partial(reduce_kernel, grp_size, pix_size),
        out_shape=jax.ShapeDtypeStruct(shape, jnp.float32),
        in_specs=[pl.BlockSpec(memory_space=pltpu.VMEM)],
        out_specs=pl.BlockSpec(memory_space=pltpu.VMEM),
        scratch_shapes=[pltpu.VMEM(shape, jnp.float32), pltpu.SemaphoreType.DMA((4, total))],
        compiler_params=pltpu.CompilerParams(collective_id=0, has_side_effects=True),
    )(packed.reshape(shape))
    return out.reshape(rows, columns)


def pack_gram(real, imag):
    size = real.shape[0]
    row = lax.broadcasted_iota(jnp.int32, (size, size), 0)
    column = lax.broadcasted_iota(jnp.int32, (size, size), 1)
    return jnp.where(row <= column, real, imag)


def modes_kernel(packed, start, group, owned, modes, power, weights, inverse):
    highest = lax.Precision.HIGHEST
    size = packed.shape[0]
    rank = start.shape[0]

    @pl.when(pl.program_id(0) == 0)
    def _():
        values = packed[...]
        row = lax.broadcasted_iota(jnp.int32, (size, size), 0)
        column = lax.broadcasted_iota(jnp.int32, (size, size), 1)
        turned = values.T
        real = jnp.where(row <= column, values, turned)
        imag = jnp.where(row > column, values, jnp.where(row < column, -turned, 0.0))
        gram = jnp.concatenate(
            [jnp.concatenate([real, -imag], axis=1), jnp.concatenate([imag, real], axis=1)], axis=0
        )
        basis = start[...]
        for _ in range(STEPS):
            image = jnp.dot(basis, gram, precision=highest, preferred_element_type=jnp.float32)
            basis = image / jnp.sqrt(jnp.sum(image * image, axis=1, keepdims=True) + 1e-06)
        rounded = basis.astype(jnp.bfloat16)
        coeff = rounded.astype(jnp.float32)
        weighted = jnp.dot(coeff, gram, precision=highest, preferred_element_type=jnp.float32)
        energy = jnp.sum(coeff * weighted, axis=1, keepdims=True)
        trace = jnp.sum(jnp.where(row == column, values, 0.0))
        power[...] = energy * size / trace
        scale = lax.rsqrt(energy / (NROW * NCOL) + 1e-06)
        inverse[...] = jnp.concatenate([scale, scale], axis=0)
        half = size // 2
        swap = group[0] == 1

        def local_order(block):
            return jnp.where(swap, jnp.concatenate([block[:, half:], block[:, :half]], axis=1), block)

        real_part = local_order(coeff[:, :size])
        imag_part = local_order(coeff[:, size:])
        weights[...] = jnp.concatenate(
            [
                jnp.concatenate([real_part, -imag_part], axis=1),
                jnp.concatenate([imag_part, real_part], axis=1),
            ],
            axis=0,
        ).astype(jnp.bfloat16)

    for step in range(owned.shape[1]):
        block = jnp.concatenate([owned[0, step], owned[1, step]], axis=0)
        product = jnp.dot(weights[...], block, preferred_element_type=jnp.float32) * inverse[...]
        product = product.astype(jnp.bfloat16)
        modes[0, step] = product[:rank]
        modes[1, step] = product[rank:]


def make_modes(packed, start_basis, group_index, owned):
    _, count, slots, pixels = owned.shape
    rank = start_basis.shape[2]
    tile = math.gcd(count, 8)
    start = jnp.concatenate([start_basis[0].T, start_basis[1].T], axis=1)
    modes, power = pl.pallas_call(
        modes_kernel,
        grid=(count // tile,),
        out_shape=(
            jax.ShapeDtypeStruct((2, count, rank, pixels), jnp.bfloat16),
            jax.ShapeDtypeStruct((rank, 1), jnp.float32),
        ),
        in_specs=[
            pl.BlockSpec((slots, slots), lambda i: (0, 0)),
            pl.BlockSpec((rank, 2 * slots), lambda i: (0, 0)),
            pl.BlockSpec(memory_space=pltpu.SMEM),
            pl.BlockSpec((2, tile, slots, pixels), lambda i: (0, i, 0, 0)),
        ],
        out_specs=(
            pl.BlockSpec((2, tile, rank, pixels), lambda i: (0, i, 0, 0)),
            pl.BlockSpec((rank, 1), lambda i: (0, 0)),
        ),
        scratch_shapes=[
            pltpu.VMEM((2 * rank, 2 * slots), jnp.bfloat16),
            pltpu.VMEM((2 * rank, 1), jnp.float32),
        ],
        compiler_params=pltpu.CompilerParams(vmem_limit_bytes=32 * 1024 * 1024),
    )(packed, start, group_index.reshape(1), owned)
    return modes, power.reshape(rank)


def local(fields, lens_phase, occupancy, focus_scale, assignment, start_basis):
    local_fields = fields[0]
    modes = local_fields.shape[1]
    group_index = lax.axis_index("grp")
    electron = lax.dynamic_slice_in_dim(assignment, group_index * modes, modes)
    choose = (
        electron[:, None] == jnp.arange(assignment.shape[0], dtype=jnp.int32)[None, :]
    ).astype(jnp.float32)
    amplitude = jnp.sqrt(jnp.sum(choose * occupancy[None, :], axis=1))[:, None, None]
    chromatic = jnp.sum(choose * focus_scale[None, :], axis=1)
    angle = chromatic[:, None, None] * lens_phase[None]
    cosine = jnp.cos(angle)
    sine = jnp.sin(angle)
    field_re = local_fields[0].astype(jnp.float32)
    field_im = local_fields[1].astype(jnp.float32)
    phased = jnp.stack(
        [
            amplitude * (field_re * cosine - field_im * sine),
            amplitude * (field_re * sine + field_im * cosine),
        ]
    ).astype(jnp.bfloat16)
    cos_cols, sin_cols = dft_tables(lens_phase.shape[1])
    col_cos = jnp.einsum("zmrc,ck->zmkr", phased, cos_cols, preferred_element_type=jnp.float32)
    col_sin = jnp.einsum("zmrc,ck->zmkr", phased, sin_cols, preferred_element_type=jnp.float32)
    across = jnp.stack([col_cos[0] + col_sin[1], col_cos[1] - col_sin[0]]).astype(jnp.bfloat16)
    full_rows = across.shape[3] * lax.axis_size("pix")
    cos_rows, sin_rows = dft_tables(full_rows)
    pieces = lax.all_to_all(across, "pix", split_axis=2, concat_axis=3, tiled=True)
    half_rows = full_rows // lax.axis_size("grp")
    cos_rows = jnp.roll(cos_rows, -group_index * half_rows, axis=1)
    sin_rows = jnp.roll(sin_rows, -group_index * half_rows, axis=1)

    def row_transform(first):
        cos_part = cos_rows[:, first:first + half_rows]
        sin_part = sin_rows[:, first:first + half_rows]
        row_cos = jnp.dot(pieces, cos_part, preferred_element_type=jnp.float32)
        row_sin = jnp.dot(pieces, sin_part, preferred_element_type=jnp.float32)
        return jnp.stack([row_cos[0] + row_sin[1], row_cos[1] - row_sin[0]]).astype(jnp.bfloat16)

    stack_size = modes * lax.axis_size("grp")
    partner = partner_2(row_transform(half_rows), "grp", 0)
    owned = jnp.concatenate([row_transform(0), partner], axis=1)
    flat = owned.reshape(2, stack_size, -1)
    blocks = jnp.einsum("xap,ybp->xyab", flat, flat, preferred_element_type=jnp.float32)
    local_re = blocks[0, 0] + blocks[1, 1]
    local_im = blocks[0, 1] - blocks[1, 0]

    packed = jnp.where(
        group_index == 0,
        pack_gram(local_re, local_im),
        pack_gram(
            jnp.roll(local_re, (modes, modes), (0, 1)), jnp.roll(local_im, (modes, modes), (0, 1))
        ),
    )
    packed = sum_over_devices(packed)
    coherent_modes, relative_power = make_modes(
        packed, start_basis, group_index, jnp.swapaxes(owned, 1, 2)
    )
    return (jnp.swapaxes(coherent_modes, 1, 2), relative_power)


def solution(mesh):
    in_specs = (P("grp", None, None, "pix", None), P("pix", None), P(), P(), P(), P())
    out_specs = (P(None, None, "pix", "grp"), P())
    return jax.shard_map(local, mesh=mesh, in_specs=in_specs, out_specs=out_specs, check_vma=False)
```

```python
import functools
import math

import jax
import jax.numpy as jnp
from jax import lax
from jax.experimental import pallas as pl
from jax.experimental.pallas import tpu as pltpu
from jax.sharding import PartitionSpec as P

NROW = 512
NCOL = 512
STEPS = 2
CHUNKS = 4


def partner_2(array, axis, apart):
    return lax.ppermute(array, axis, [(i, i ^ 1 << apart) for i in range(lax.axis_size(axis))])


def dft_tables(length):
    index = jnp.arange(length, dtype=jnp.int32)
    product = index[:, None] * index[None, :] % length
    angle = product.astype(jnp.float32) * (2.0 * math.pi / length)
    factor = 1.0 / math.sqrt(length)
    return (
        (jnp.cos(angle) * factor).astype(jnp.bfloat16),
        (jnp.sin(angle) * factor).astype(jnp.bfloat16),
    )


MESH = pl.DeviceIdType.MESH


def place(flat, pix_size):
    return (flat // pix_size, lax.rem(flat, pix_size))


def greet(me, total, pix_size):
    barrier = pltpu.get_barrier_semaphore()

    def hello(step, carry):
        other = lax.rem(me + step, total)
        pl.semaphore_signal(barrier, inc=1, device_id=place(other, pix_size), device_id_type=MESH)
        return carry

    lax.fori_loop(1, total, hello, 0)
    pl.semaphore_wait(barrier, total - 1)


def all_reduce(me, total, pix_size, part, landed, result, sems):
    def scatter(step):
        other = lax.rem(me + step, total)
        return pltpu.make_async_remote_copy(
            src_ref=part.at[other],
            dst_ref=landed.at[step],
            send_sem=sems.at[0, step],
            recv_sem=sems.at[1, step],
            device_id=place(other, pix_size),
            device_id_type=MESH,
        )

    def gather(step):
        other = lax.rem(me + step, total)
        return pltpu.make_async_remote_copy(
            src_ref=result.at[me],
            dst_ref=result.at[me],
            send_sem=sems.at[2, step],
            recv_sem=sems.at[3, step],
            device_id=place(other, pix_size),
            device_id_type=MESH,
        )

    def start_scatter(step, carry):
        scatter(step).start()
        return carry

    def add_one(step, sum_so_far):
        scatter(step).wait_recv()
        return sum_so_far + landed[step]

    def start_gather(step, carry):
        gather(step).start()
        return carry

    def finish(step, carry):
        scatter(step).wait_send()
        gather(step).wait_send()
        source = lax.rem(me - step + total, total)
        pltpu.make_async_remote_copy(
            src_ref=result.at[me],
            dst_ref=result.at[source],
            send_sem=sems.at[2, step],
            recv_sem=sems.at[3, step],
            device_id=place(source, pix_size),
            device_id_type=MESH,
        ).wait_recv()
        return carry

    lax.fori_loop(1, total, start_scatter, 0)
    result[me] = lax.fori_loop(1, total, add_one, part[me])
    lax.fori_loop(1, total, start_gather, 0)
    lax.fori_loop(1, total, finish, 0)


def reduce_kernel(grp_size, pix_size, part, result, landed, sems):
    total = grp_size * pix_size
    me = lax.axis_index("grp") * pix_size + lax.axis_index("pix")
    greet(me, total, pix_size)
    all_reduce(me, total, pix_size, part, landed, result, sems)


def sum_over_devices(packed):
    grp_size, pix_size = lax.axis_size("grp"), lax.axis_size("pix")
    total = grp_size * pix_size
    rows, columns = packed.shape
    shape = (total, rows // total, columns)
    out = pl.pallas_call(
        functools.partial(reduce_kernel, grp_size, pix_size),
        out_shape=jax.ShapeDtypeStruct(shape, jnp.float32),
        in_specs=[pl.BlockSpec(memory_space=pltpu.VMEM)],
        out_specs=pl.BlockSpec(memory_space=pltpu.VMEM),
        scratch_shapes=[pltpu.VMEM(shape, jnp.float32), pltpu.SemaphoreType.DMA((4, total))],
        compiler_params=pltpu.CompilerParams(collective_id=0, has_side_effects=True),
    )(packed.reshape(shape))
    return out.reshape(rows, columns)


def pack_gram(real, imag):
    size = real.shape[0]
    row = lax.broadcasted_iota(jnp.int32, (size, size), 0)
    column = lax.broadcasted_iota(jnp.int32, (size, size), 1)
    return jnp.where(row <= column, real, imag)


def modes_kernel(packed, start, group, *rest):
    *owned_chunks, modes, power, weights, inverse = rest
    highest = lax.Precision.HIGHEST
    size = packed.shape[0]
    rank = start.shape[0]

    @pl.when(pl.program_id(0) == 0)
    def _():
        values = packed[...]
        row = lax.broadcasted_iota(jnp.int32, (size, size), 0)
        column = lax.broadcasted_iota(jnp.int32, (size, size), 1)
        turned = values.T
        real = jnp.where(row <= column, values, turned)
        imag = jnp.where(row > column, values, jnp.where(row < column, -turned, 0.0))
        gram = jnp.concatenate(
            [jnp.concatenate([real, -imag], axis=1), jnp.concatenate([imag, real], axis=1)], axis=0
        )
        basis = start[...]
        for _ in range(STEPS):
            image = jnp.dot(basis, gram, precision=highest, preferred_element_type=jnp.float32)
            basis = image / jnp.sqrt(jnp.sum(image * image, axis=1, keepdims=True) + 1e-06)
        rounded = basis.astype(jnp.bfloat16)
        coeff = rounded.astype(jnp.float32)
        weighted = jnp.dot(coeff, gram, precision=highest, preferred_element_type=jnp.float32)
        energy = jnp.sum(coeff * weighted, axis=1, keepdims=True)
        trace = jnp.sum(jnp.where(row == column, values, 0.0))
        power[...] = energy * size / trace
        scale = lax.rsqrt(energy / (NROW * NCOL) + 1e-06)
        inverse[...] = jnp.concatenate([scale, scale], axis=0)
        half = size // 2
        swap = group[0] == 1

        def local_order(block):
            return jnp.where(swap, jnp.concatenate([block[:, half:], block[:, :half]], axis=1), block)

        real_part = local_order(coeff[:, :size])
        imag_part = local_order(coeff[:, size:])
        weights[...] = jnp.concatenate(
            [
                jnp.concatenate([real_part, -imag_part], axis=1),
                jnp.concatenate([imag_part, real_part], axis=1),
            ],
            axis=0,
        ).astype(jnp.bfloat16)

    for chunk, owned in enumerate(owned_chunks):
        for step in range(owned.shape[1]):
            block = jnp.concatenate([owned[0, step], owned[1, step]], axis=0)
            product = jnp.dot(weights[...], block, preferred_element_type=jnp.float32)
            product = (product * inverse[...]).astype(jnp.bfloat16)
            modes[0, chunk, step] = product[:rank]
            modes[1, chunk, step] = product[rank:]


def make_modes(packed, start_basis, group_index, owned_chunks):
    _, count, slots, pixels = owned_chunks[0].shape
    chunks = len(owned_chunks)
    rank = start_basis.shape[2]
    tile = math.gcd(count, 2)
    start = jnp.concatenate([start_basis[0].T, start_basis[1].T], axis=1)
    modes, power = pl.pallas_call(
        modes_kernel,
        grid=(count // tile,),
        out_shape=(
            jax.ShapeDtypeStruct((2, chunks, count, rank, pixels), jnp.bfloat16),
            jax.ShapeDtypeStruct((rank, 1), jnp.float32),
        ),
        in_specs=[
            pl.BlockSpec((slots, slots), lambda i: (0, 0)),
            pl.BlockSpec((rank, 2 * slots), lambda i: (0, 0)),
            pl.BlockSpec(memory_space=pltpu.SMEM),
        ]
        + [pl.BlockSpec((2, tile, slots, pixels), lambda i: (0, i, 0, 0))] * chunks,
        out_specs=(
            pl.BlockSpec((2, chunks, tile, rank, pixels), lambda i: (0, 0, i, 0, 0)),
            pl.BlockSpec((rank, 1), lambda i: (0, 0)),
        ),
        scratch_shapes=[
            pltpu.VMEM((2 * rank, 2 * slots), jnp.bfloat16),
            pltpu.VMEM((2 * rank, 1), jnp.float32),
        ],
        compiler_params=pltpu.CompilerParams(vmem_limit_bytes=32 * 1024 * 1024),
    )(packed, start, group_index.reshape(1), *owned_chunks)
    return modes.reshape(2, chunks * count, rank, pixels), power.reshape(rank)


def cos_sin(angle):
    turns = jnp.round(angle * (0.5 / math.pi))
    high = 6.28125
    reduced = (angle - turns * high) - turns * (2.0 * math.pi - high)
    quarter = reduced * 0.25
    square = quarter * quarter
    sine = quarter * (1.0 + square * (-1 / 6 + square * (1 / 120 + square * (-1 / 5040 + square / 362880))))
    cosine = 1.0 + square * (-0.5 + square * (1 / 24 + square * (-1 / 720 + square / 40320)))
    half_sine = 2.0 * sine * cosine
    half_cosine = 1.0 - 2.0 * sine * sine
    return 1.0 - 2.0 * half_sine * half_sine, 2.0 * half_sine * half_cosine


def local(fields, lens_phase, occupancy, focus_scale, assignment, start_basis):
    local_fields = fields[0]
    modes = local_fields.shape[1]
    group_index = lax.axis_index("grp")
    electron = lax.dynamic_slice_in_dim(assignment, group_index * modes, modes)
    choose = (
        electron[:, None] == jnp.arange(assignment.shape[0], dtype=jnp.int32)[None, :]
    ).astype(jnp.float32)
    amplitude = jnp.sqrt(jnp.sum(choose * occupancy[None, :], axis=1))[:, None, None]
    chromatic = jnp.sum(choose * focus_scale[None, :], axis=1)
    angle = chromatic[:, None, None] * lens_phase[None]
    cosine, sine = cos_sin(angle)
    field_re = local_fields[0].astype(jnp.float32)
    field_im = local_fields[1].astype(jnp.float32)
    phased = jnp.stack(
        [
            amplitude * (field_re * cosine - field_im * sine),
            amplitude * (field_re * sine + field_im * cosine),
        ]
    ).astype(jnp.bfloat16)
    cos_cols, sin_cols = dft_tables(lens_phase.shape[1])
    pix_size = lax.axis_size("pix")
    columns = lens_phase.shape[1] // pix_size
    chunks = math.gcd(columns, CHUNKS)
    full_rows = phased.shape[2] * pix_size
    cos_rows, sin_rows = dft_tables(full_rows)
    half_rows = full_rows // lax.axis_size("grp")
    cos_rows = jnp.roll(cos_rows, -group_index * half_rows, axis=1)
    sin_rows = jnp.roll(sin_rows, -group_index * half_rows, axis=1)
    stack_size = modes * lax.axis_size("grp")
    wanted = (lens_phase.shape[1], pix_size, chunks, columns // chunks)
    cos_cols = cos_cols.reshape(wanted)
    sin_cols = sin_cols.reshape(wanted)
    owned_chunks, others, partners, kept = [], [], [], []
    local_re = local_im = 0.0
    for chunk in range(chunks):
        cos_part = cos_cols[:, :, chunk].reshape(wanted[0], -1)
        sin_part = sin_cols[:, :, chunk].reshape(wanted[0], -1)
        col_cos = jnp.einsum("zmrc,ck->zmkr", phased, cos_part, preferred_element_type=jnp.float32)
        col_sin = jnp.einsum("zmrc,ck->zmkr", phased, sin_part, preferred_element_type=jnp.float32)
        across = jnp.stack([col_cos[0] + col_sin[1], col_cos[1] - col_sin[0]]).astype(jnp.bfloat16)
        if chunk >= 2:
            across, others[chunk - 2] = lax.optimization_barrier((across, others[chunk - 2]))
        if chunk >= 3:
            across, partners[chunk - 3] = lax.optimization_barrier((across, partners[chunk - 3]))
        pieces = lax.all_to_all(across, "pix", split_axis=2, concat_axis=3, tiled=True)

        def row_transform(first):
            cos_half = cos_rows[:, first:first + half_rows]
            sin_half = sin_rows[:, first:first + half_rows]
            row_cos = jnp.dot(pieces, cos_half, preferred_element_type=jnp.float32)
            row_sin = jnp.dot(pieces, sin_half, preferred_element_type=jnp.float32)
            return jnp.stack([row_cos[0] + row_sin[1], row_cos[1] - row_sin[0]]).astype(jnp.bfloat16)

        other = row_transform(half_rows)
        others.append(other)
        partners.append(partner_2(other, "grp", 0))
        kept.append(row_transform(0))
    for chunk in range(chunks):
        owned = jnp.concatenate([kept[chunk], partners[chunk]], axis=1)
        flat = owned.reshape(2, stack_size, -1)
        blocks = jnp.einsum("xap,ybp->xyab", flat, flat, preferred_element_type=jnp.float32)
        local_re += blocks[0, 0] + blocks[1, 1]
        local_im += blocks[0, 1] - blocks[1, 0]
        owned_chunks.append(jnp.swapaxes(owned, 1, 2))
    packed = jnp.where(
        group_index == 0,
        pack_gram(local_re, local_im),
        pack_gram(
            jnp.roll(local_re, (modes, modes), (0, 1)), jnp.roll(local_im, (modes, modes), (0, 1))
        ),
    )
    packed = sum_over_devices(packed)
    coherent_modes, relative_power = make_modes(packed, start_basis, group_index, owned_chunks)
    return (jnp.swapaxes(coherent_modes, 1, 2), relative_power)


def solution(mesh):
    in_specs = (P("grp", None, None, "pix", None), P("pix", None), P(), P(), P(), P())
    out_specs = (P(None, None, "pix", "grp"), P())
    return jax.shard_map(local, mesh=mesh, in_specs=in_specs, out_specs=out_specs, check_vma=False)
```

```python
import functools
import math

import jax
import jax.numpy as jnp
from jax import lax
from jax.experimental import pallas as pl
from jax.experimental.pallas import tpu as pltpu
from jax.sharding import PartitionSpec as P

NROW = 512
NCOL = 512
STEPS = 2
SHARES = (1, 2, 1)


def partner_2(array, axis, apart):
    return lax.ppermute(array, axis, [(i, i ^ 1 << apart) for i in range(lax.axis_size(axis))])


def cos_sin(angle):
    turns = jnp.round(angle * (0.5 / math.pi))
    high = 6.28125
    reduced = (angle - turns * high) - turns * (2.0 * math.pi - high)
    quarter = reduced * 0.25
    square = quarter * quarter
    sine = quarter * (1.0 + square * (-1 / 6 + square * (1 / 120 + square * (-1 / 5040 + square / 362880))))
    cosine = 1.0 + square * (-0.5 + square * (1 / 24 + square * (-1 / 720 + square / 40320)))
    half_sine = 2.0 * sine * cosine
    half_cosine = 1.0 - 2.0 * sine * sine
    return 1.0 - 2.0 * half_sine * half_sine, 2.0 * half_sine * half_cosine


def dft_tables(length):
    index = jnp.arange(length, dtype=jnp.int32)
    product = index[:, None] * index[None, :] % length
    angle = product.astype(jnp.float32) * (2.0 * math.pi / length)
    factor = 1.0 / math.sqrt(length)
    cosine, sine = cos_sin(angle)
    return ((cosine * factor).astype(jnp.bfloat16), (sine * factor).astype(jnp.bfloat16))


MESH = pl.DeviceIdType.MESH


def place(flat, pix_size):
    return (flat // pix_size, lax.rem(flat, pix_size))


def greet(me, total, pix_size):
    barrier = pltpu.get_barrier_semaphore()

    def hello(step, carry):
        other = lax.rem(me + step, total)
        pl.semaphore_signal(barrier, inc=1, device_id=place(other, pix_size), device_id_type=MESH)
        return carry

    lax.fori_loop(1, total, hello, 0)
    pl.semaphore_wait(barrier, total - 1)


def all_reduce(me, total, pix_size, part, landed, result, sems):
    def scatter(step):
        other = lax.rem(me + step, total)
        return pltpu.make_async_remote_copy(
            src_ref=part.at[other],
            dst_ref=landed.at[step],
            send_sem=sems.at[0, step],
            recv_sem=sems.at[1, step],
            device_id=place(other, pix_size),
            device_id_type=MESH,
        )

    def gather(step):
        other = lax.rem(me + step, total)
        return pltpu.make_async_remote_copy(
            src_ref=result.at[me],
            dst_ref=result.at[me],
            send_sem=sems.at[2, step],
            recv_sem=sems.at[3, step],
            device_id=place(other, pix_size),
            device_id_type=MESH,
        )

    def start_scatter(step, carry):
        scatter(step).start()
        return carry

    def add_one(step, sum_so_far):
        scatter(step).wait_recv()
        return sum_so_far + landed[step]

    def start_gather(step, carry):
        gather(step).start()
        return carry

    def finish(step, carry):
        scatter(step).wait_send()
        gather(step).wait_send()
        source = lax.rem(me - step + total, total)
        pltpu.make_async_remote_copy(
            src_ref=result.at[me],
            dst_ref=result.at[source],
            send_sem=sems.at[2, step],
            recv_sem=sems.at[3, step],
            device_id=place(source, pix_size),
            device_id_type=MESH,
        ).wait_recv()
        return carry

    lax.fori_loop(1, total, start_scatter, 0)
    result[me] = lax.fori_loop(1, total, add_one, part[me])
    lax.fori_loop(1, total, start_gather, 0)
    lax.fori_loop(1, total, finish, 0)


def reduce_kernel(grp_size, pix_size, part, result, landed, sems):
    total = grp_size * pix_size
    me = lax.axis_index("grp") * pix_size + lax.axis_index("pix")
    greet(me, total, pix_size)
    all_reduce(me, total, pix_size, part, landed, result, sems)


def sum_over_devices(packed):
    grp_size, pix_size = lax.axis_size("grp"), lax.axis_size("pix")
    total = grp_size * pix_size
    rows, columns = packed.shape
    shape = (total, rows // total, columns)
    out = pl.pallas_call(
        functools.partial(reduce_kernel, grp_size, pix_size),
        out_shape=jax.ShapeDtypeStruct(shape, jnp.float32),
        in_specs=[pl.BlockSpec(memory_space=pltpu.VMEM)],
        out_specs=pl.BlockSpec(memory_space=pltpu.VMEM),
        scratch_shapes=[pltpu.VMEM(shape, jnp.float32), pltpu.SemaphoreType.DMA((4, total))],
        compiler_params=pltpu.CompilerParams(collective_id=0, has_side_effects=True),
    )(packed.reshape(shape))
    return out.reshape(rows, columns)


def pack_gram(real, imag):
    size = real.shape[0]
    row = lax.broadcasted_iota(jnp.int32, (size, size), 0)
    column = lax.broadcasted_iota(jnp.int32, (size, size), 1)
    return jnp.where(row <= column, real, imag)


def modes_kernel(packed, start, group, *rest):
    *owned_chunks, modes, power, weights, inverse = rest
    highest = lax.Precision.HIGHEST
    size = packed.shape[0]
    rank = start.shape[0]

    @pl.when(pl.program_id(0) == 0)
    def _():
        values = packed[...]
        row = lax.broadcasted_iota(jnp.int32, (size, size), 0)
        column = lax.broadcasted_iota(jnp.int32, (size, size), 1)
        turned = values.T
        real = jnp.where(row <= column, values, turned)
        imag = jnp.where(row > column, values, jnp.where(row < column, -turned, 0.0))
        gram = jnp.concatenate(
            [jnp.concatenate([real, -imag], axis=1), jnp.concatenate([imag, real], axis=1)], axis=0
        )
        basis = start[...]
        for _ in range(STEPS):
            image = jnp.dot(basis, gram, precision=highest, preferred_element_type=jnp.float32)
            basis = image / jnp.sqrt(jnp.sum(image * image, axis=1, keepdims=True) + 1e-06)
        rounded = basis.astype(jnp.bfloat16)
        coeff = rounded.astype(jnp.float32)
        weighted = jnp.dot(coeff, gram, precision=highest, preferred_element_type=jnp.float32)
        energy = jnp.sum(coeff * weighted, axis=1, keepdims=True)
        trace = jnp.sum(jnp.where(row == column, values, 0.0))
        power[...] = energy * size / trace
        scale = lax.rsqrt(energy / (NROW * NCOL) + 1e-06)
        inverse[...] = jnp.concatenate([scale, scale], axis=0)
        half = size // 2
        swap = group[0] == 1

        def local_order(block):
            return jnp.where(swap, jnp.concatenate([block[:, half:], block[:, :half]], axis=1), block)

        real_part = local_order(coeff[:, :size])
        imag_part = local_order(coeff[:, size:])
        weights[...] = jnp.concatenate(
            [
                jnp.concatenate([real_part, -imag_part], axis=1),
                jnp.concatenate([imag_part, real_part], axis=1),
            ],
            axis=0,
        ).astype(jnp.bfloat16)

    for chunk, owned in enumerate(owned_chunks):
        for step in range(owned.shape[1]):
            block = jnp.concatenate([owned[0, step], owned[1, step]], axis=0)
            product = jnp.dot(weights[...], block, preferred_element_type=jnp.float32)
            product = (product * inverse[...]).astype(jnp.bfloat16)
            modes[0, chunk, step] = product[:rank]
            modes[1, chunk, step] = product[rank:]


def shifted(offset, index):
    return (0, index + offset, 0, 0)


def make_modes(packed, start_basis, group_index, owned_chunks, shares):
    slots, pixels = owned_chunks[0].shape[2:]
    count = owned_chunks[0].shape[1] // shares[0]
    chunks = sum(shares)
    rank = start_basis.shape[2]
    tile = math.gcd(count, 2)
    start = jnp.concatenate([start_basis[0].T, start_basis[1].T], axis=1)
    repeated = [owned for owned, share in zip(owned_chunks, shares) for _ in range(share)]
    modes, power = pl.pallas_call(
        modes_kernel,
        grid=(count // tile,),
        out_shape=(
            jax.ShapeDtypeStruct((2, chunks, count, rank, pixels), jnp.bfloat16),
            jax.ShapeDtypeStruct((rank, 1), jnp.float32),
        ),
        in_specs=[
            pl.BlockSpec((slots, slots), lambda i: (0, 0)),
            pl.BlockSpec((rank, 2 * slots), lambda i: (0, 0)),
            pl.BlockSpec(memory_space=pltpu.SMEM),
        ]
        + [
            pl.BlockSpec(
                (2, tile, slots, pixels), functools.partial(shifted, part * (count // tile))
            )
            for share in shares
            for part in range(share)
        ],
        out_specs=(
            pl.BlockSpec((2, chunks, tile, rank, pixels), lambda i: (0, 0, i, 0, 0)),
            pl.BlockSpec((rank, 1), lambda i: (0, 0)),
        ),
        scratch_shapes=[
            pltpu.VMEM((2 * rank, 2 * slots), jnp.bfloat16),
            pltpu.VMEM((2 * rank, 1), jnp.float32),
        ],
        compiler_params=pltpu.CompilerParams(vmem_limit_bytes=32 * 1024 * 1024),
    )(packed, start, group_index.reshape(1), *repeated)
    return modes.reshape(2, chunks * count, rank, pixels), power.reshape(rank)


def local(fields, lens_phase, occupancy, focus_scale, assignment, start_basis):
    local_fields = fields[0]
    modes = local_fields.shape[1]
    group_index = lax.axis_index("grp")
    electron = lax.dynamic_slice_in_dim(assignment, group_index * modes, modes)
    choose = (
        electron[:, None] == jnp.arange(assignment.shape[0], dtype=jnp.int32)[None, :]
    ).astype(jnp.float32)
    amplitude = jnp.sqrt(jnp.sum(choose * occupancy[None, :], axis=1))[:, None, None]
    chromatic = jnp.sum(choose * focus_scale[None, :], axis=1)
    angle = chromatic[:, None, None] * lens_phase[None]
    cosine, sine = cos_sin(angle)
    field_re = local_fields[0].astype(jnp.float32)
    field_im = local_fields[1].astype(jnp.float32)
    phased = jnp.stack(
        [
            amplitude * (field_re * cosine - field_im * sine),
            amplitude * (field_re * sine + field_im * cosine),
        ]
    ).astype(jnp.bfloat16)
    cos_cols, sin_cols = dft_tables(lens_phase.shape[1])
    pix_size = lax.axis_size("pix")
    columns = lens_phase.shape[1] // pix_size
    units = sum(SHARES) if columns % sum(SHARES) == 0 else 1
    shares = SHARES if units > 1 else (1,)
    chunks = len(shares)
    unit = columns // units
    full_rows = phased.shape[2] * pix_size
    cos_rows, sin_rows = dft_tables(full_rows)
    half_rows = full_rows // lax.axis_size("grp")
    cos_rows = jnp.roll(cos_rows, -group_index * half_rows, axis=1)
    sin_rows = jnp.roll(sin_rows, -group_index * half_rows, axis=1)
    stack_size = modes * lax.axis_size("grp")
    wanted = (lens_phase.shape[1], pix_size, columns)
    cos_cols = cos_cols.reshape(wanted)
    sin_cols = sin_cols.reshape(wanted)
    owned_chunks, partners, kept = [], [], []
    local_re = local_im = 0.0
    for chunk in range(chunks):
        begin, end = sum(shares[:chunk]) * unit, sum(shares[:chunk + 1]) * unit
        cos_part = cos_cols[:, :, begin:end].reshape(wanted[0], -1)
        sin_part = sin_cols[:, :, begin:end].reshape(wanted[0], -1)
        col_cos = jnp.einsum("zmrc,ck->zmkr", phased, cos_part, preferred_element_type=jnp.float32)
        col_sin = jnp.einsum("zmrc,ck->zmkr", phased, sin_part, preferred_element_type=jnp.float32)
        across = jnp.stack([col_cos[0] + col_sin[1], col_cos[1] - col_sin[0]]).astype(jnp.bfloat16)
        if chunk >= 2:
            across, partners[chunk - 2] = lax.optimization_barrier((across, partners[chunk - 2]))
        pieces = lax.all_to_all(across, "pix", split_axis=2, concat_axis=3, tiled=True)

        def row_transform(first):
            cos_half = cos_rows[:, first:first + half_rows]
            sin_half = sin_rows[:, first:first + half_rows]
            row_cos = jnp.dot(pieces, cos_half, preferred_element_type=jnp.float32)
            row_sin = jnp.dot(pieces, sin_half, preferred_element_type=jnp.float32)
            return jnp.stack([row_cos[0] + row_sin[1], row_cos[1] - row_sin[0]]).astype(jnp.bfloat16)

        partners.append(partner_2(row_transform(half_rows), "grp", 0))
        kept.append(row_transform(0))
    for chunk in range(chunks):
        owned = jnp.concatenate([kept[chunk], partners[chunk]], axis=1)
        flat = owned.reshape(2, stack_size, -1)
        blocks = jnp.einsum("xap,ybp->xyab", flat, flat, preferred_element_type=jnp.float32)
        local_re += blocks[0, 0] + blocks[1, 1]
        local_im += blocks[0, 1] - blocks[1, 0]
        owned_chunks.append(jnp.swapaxes(owned, 1, 2))
    packed = jnp.where(
        group_index == 0,
        pack_gram(local_re, local_im),
        pack_gram(
            jnp.roll(local_re, (modes, modes), (0, 1)), jnp.roll(local_im, (modes, modes), (0, 1))
        ),
    )
    packed = sum_over_devices(packed)
    coherent_modes, relative_power = make_modes(
        packed, start_basis, group_index, owned_chunks, shares
    )
    return (jnp.swapaxes(coherent_modes, 1, 2), relative_power)


def solution(mesh):
    in_specs = (P("grp", None, None, "pix", None), P("pix", None), P(), P(), P(), P())
    out_specs = (P(None, None, "pix", "grp"), P())
    return jax.shard_map(local, mesh=mesh, in_specs=in_specs, out_specs=out_specs, check_vma=False)
```
